32 devices in a mesh: groups: 2 (over y), kv: 16 (over z, x, core).
Axes of the slice: x: 2, y: 2, z: 4, core: 2. Of those that a mesh axis runs over, the one named last changes fastest.
Arguments:
- queries: bfloat16 [2, 1024, 4096], P(None, ('groups', 'kv')), parts along dimension 1, as said below
- shared_prefix_keys: bfloat16 [16384, 512], P('kv'), may hold values from -6 to 6
- shared_prefix_values: bfloat16 [16384, 512], P('kv'), may hold values from -6 to 6
- row_suffix_keys: bfloat16 [1024, 32, 512], P(('groups', 'kv')), parts along dimension 0, may hold values from -6 to 6
- row_suffix_values: bfloat16 [1024, 32, 512], P(('groups', 'kv')), parts along dimension 0, may hold values from -6 to 6
- step_keys: bfloat16 [2, 1024, 512], P(None, ('groups', 'kv')), parts along dimension 1, may hold values from -6 to 6
- step_values: bfloat16 [2, 1024, 512], P(None, ('groups', 'kv')), parts along dimension 1, may hold values from -6 to 6
- tree_blocks: int32 [1024, 4], P(('groups', 'kv')), parts along dimension 0, may hold values from 0 to 15, all different within a row; in each aligned block of 32 rows (0 to 31, 32 to 63, ...) at most 16 rows name the same one
- block_slot: int32 [16], replicated, may hold values from 0 to 15, each once
- suffix_length: int32 [1024], P(('groups', 'kv')), parts along dimension 0, may hold values from 1 to 32, as said below
Outputs:
- attended: bfloat16 [2, 1024, 4096], P(None, ('groups', 'kv')), parts along dimension 1
The draws below stay inside these ranges and needn't reach their ends.
There are 2 independent parts, one for each index of `groups`. The reference program is written for one: setup_inputs(seed, part) draws one part's arguments, and reference() takes and returns one part's arrays. A program takes and returns all parts, laid end to end along the dimension named above; an argument that names none is the same for every part. Nothing has to cross between parts.
Inputs may be any that keep to these rules, and one draw needn't show every extreme that they name: `tree_blocks`: each row lists 4 different tree blocks; among the rows of one kv index no block is listed by more than 16 rows, and some block by exactly 16. A permutation: tree block b lies in slot block_slot[b]. `suffix_length`: some row holds 32 cached positions and some row one. Real-valued queries.
All inputs are finite; a program needn't handle non-finite values.
Results may differ from the reference program's by a relative error of at most 0.0057.
Values may be sent and summed in bfloat16 or wider, within the bound.
A program may use at most 128 MiB of HBM per device.

```python
import math
import jax
import jax.numpy as jnp
import numpy as np
from jax import lax

QUERY_HEADS = 32
KEY_VALUE_HEADS = 4
HEAD_SIZE = 128
BLOCK_TOKENS = 1024
PATH_BLOCKS = 4
SUFFIX_SLOTS = 32
DECODE_STEPS = 2
ROWS_DEV = 32
DECODE_ROWS = 512
PREFIX_TOKENS = 16384
CAP = 16
N_KV = 16


def draw_queries(key, part):
    first = jax.random.fold_in(key, 0)
    values = jnp.clip(jax.random.normal(first, (DECODE_STEPS, DECODE_ROWS, QUERY_HEADS * HEAD_SIZE), jnp.float32), -6.0, 6.0)
    return values.astype(jnp.bfloat16)


def draw_suffix_length(key, part):
    lengths = jax.random.randint(key, (DECODE_ROWS,), 1, SUFFIX_SLOTS + 1, dtype=jnp.int32)
    return lengths.at[0].set(SUFFIX_SLOTS).at[1].set(1)


def level_of(rng, extent, cuts, smallest, largest):
    gain, own = 1.0, jax.random.fold_in(rng, 6)
    for axis_at, shards_of in cuts:
        heights = jnp.exp(jax.random.uniform(jax.random.fold_in(own, axis_at), (shards_of,), jnp.float32, smallest / len(cuts), largest / len(cuts)))
        gain = gain * jnp.repeat(heights, extent[axis_at] // shards_of).reshape([-1 if axis == axis_at else 1 for axis in range(len(extent))])
    return gain


def assign_block(own_key, own, number, rows, count, top, reach, slope):
    order = jax.random.permutation(own_key, count)
    heavy_load, ordinary = load_shares(count, rows * top, reach, slope, True), load_shares(count, rows * top, reach, slope, False)
    places = jnp.arange(count)

    def named(sizes, turn):
        used = int((sizes > 0).sum())
        fixed = max(1, used // 4)
        shifted = fixed + (places - fixed + turn * (used - fixed)) % max(1, count - fixed)
        return jnp.zeros((count,), jnp.int32).at[order[jnp.where(places < fixed, places, shifted)]].set(jnp.asarray(sizes, jnp.int32))

    sizes = jnp.where(number % 4 == 0, named(heavy_load, number // 4), named(ordinary, number - number // 4 - 1))
    mixed = jax.random.permutation(jax.random.fold_in(own, 3), count)
    donor, taker = mixed[0:count // 2 * 2:2], mixed[1:count // 2 * 2:2]
    slack = jnp.minimum(sizes[donor] - 1, reach - sizes[taker]) // 2
    slack = jnp.where((donor == order[0]) | (taker == order[0]) | (sizes[taker] == 0), 0, jnp.maximum(slack, 0))
    shifted = jax.random.randint(jax.random.fold_in(own, 4), (count // 2,), 0, 1 << 20) % (slack + 1)
    sizes = sizes.at[donor].add(-shifted).at[taker].add(shifted)
    items = jnp.searchsorted(jnp.cumsum(sizes), jnp.arange(rows * top), side="right").astype(jnp.int32)
    table = items.reshape(top, rows).T
    table = table[jax.random.permutation(jax.random.fold_in(own, 1), rows)]
    turn = jax.random.randint(jax.random.fold_in(own, 2), (rows, 1), 0, top)
    return jnp.take_along_axis(table, (jnp.arange(top)[None, :] + turn) % top, axis=1)


def load_shares(count, total, bound, lean, full):
    weights = [(1 << 20) // math.isqrt(grade ** lean) + 1 for grade in range(1, count + 1)]
    largest = bound if full else min(bound, max(-(-total // count), total * weights[0] // sum(weights)))
    least = 1 if total - largest >= count - 1 else 0
    given, spare = [largest] + [least] * (count - 1), total - largest - least * (count - 1)
    while spare > 0:
        candidates = [i for i in range(1, count) if given[i] < largest] or [i for i in range(1, count) if given[i] < bound]
        pool, left = sum([weights[i] for i in candidates]), spare
        for i in candidates:
            addition = min(bound - given[i], max(1, left * weights[i] // pool), spare)
            given[i] = given[i] + addition
            spare = spare - addition
    return np.array(given)


def noise(rng, extent, deviation, limit, pieces=(), kind=jnp.bfloat16):
    factor_of = level_of(rng, extent, pieces, -0.22, 0.18) if pieces else 1.0
    entries = jax.random.normal(rng, extent, jnp.float32) * deviation * factor_of
    return jnp.minimum(jnp.maximum(entries, -limit), limit).astype(kind)


def setup_inputs(seed: int = 0, part: int = 0) -> dict:
    streams_of = jax.random.split(jax.random.key(seed), 11)
    part_keys = jax.random.split(jax.random.fold_in(streams_of[10], part), 11)
    queries = draw_queries(jax.random.fold_in(jax.random.fold_in(streams_of[10], part), 71), part)
    shared_prefix_keys = noise(streams_of[1], (PREFIX_TOKENS, KEY_VALUE_HEADS * HEAD_SIZE), 1.0, 6.0, ((0, 16),))
    shared_prefix_values = noise(streams_of[2], (PREFIX_TOKENS, KEY_VALUE_HEADS * HEAD_SIZE), 1.0, 6.0, ((0, 16),))
    row_suffix_keys = noise(part_keys[3], (DECODE_ROWS, SUFFIX_SLOTS, KEY_VALUE_HEADS * HEAD_SIZE), 1.0, 6.0, ((0, 16),))
    row_suffix_values = noise(part_keys[4], (DECODE_ROWS, SUFFIX_SLOTS, KEY_VALUE_HEADS * HEAD_SIZE), 1.0, 6.0, ((0, 16),))
    step_keys = noise(part_keys[5], (DECODE_STEPS, DECODE_ROWS, KEY_VALUE_HEADS * HEAD_SIZE), 1.0, 6.0, ((1, 16),))
    step_values = noise(part_keys[6], (DECODE_STEPS, DECODE_ROWS, KEY_VALUE_HEADS * HEAD_SIZE), 1.0, 6.0, ((1, 16),))
    tree_blocks_keys = jax.random.split(jax.random.fold_in(part_keys[7], 1), DECODE_ROWS // ROWS_DEV)
    tree_blocks_turns = jax.random.permutation(jax.random.fold_in(part_keys[7], 3), DECODE_ROWS // ROWS_DEV)
    tree_blocks = jax.vmap(lambda own, number: assign_block(jax.random.fold_in(part_keys[7], 2), own, number, ROWS_DEV, N_KV, PATH_BLOCKS, CAP, 2))(tree_blocks_keys, tree_blocks_turns).reshape((DECODE_ROWS, PATH_BLOCKS))
    block_slot = jax.random.permutation(streams_of[8], N_KV).astype(jnp.int32)
    suffix_length = draw_suffix_length(jax.random.fold_in(jax.random.fold_in(streams_of[10], part), 71), part)
    return dict(queries=queries, shared_prefix_keys=shared_prefix_keys, shared_prefix_values=shared_prefix_values, row_suffix_keys=row_suffix_keys, row_suffix_values=row_suffix_values, step_keys=step_keys, step_values=step_values, tree_blocks=tree_blocks, block_slot=block_slot, suffix_length=suffix_length)


NEG = -1e+30

def block_partial(query_head_rows, key_block, value_block):
    scores = jnp.einsum('bhgd,bkhd->bhgk', query_head_rows.astype(jnp.float32), key_block.astype(jnp.float32)) / math.sqrt(HEAD_SIZE)
    running_maximum = lax.optimization_barrier(jnp.max(scores, axis=-1))
    expon = jnp.exp(scores - running_maximum[..., None])
    running_total = lax.optimization_barrier(jnp.sum(expon, axis=-1))
    weights = expon.astype(jnp.bfloat16).astype(jnp.float32)
    mixed_output = jnp.einsum('bhgk,bkhd->bhgd', weights, value_block.astype(jnp.float32)) / running_total[..., None]
    return (running_maximum, running_total, mixed_output.astype(jnp.bfloat16))

def own_partial(query_head_rows, cached_key_rows, cached_value_rows, latest_keys, latest_values, lengths, step_index):
    first = jnp.einsum('bhgd,bkhd->bhgk', query_head_rows.astype(jnp.float32), cached_key_rows.astype(jnp.float32)) / math.sqrt(HEAD_SIZE)
    valid = jnp.arange(SUFFIX_SLOTS, dtype=jnp.int32)[None, None, None, :] < lengths[:, None, None, None]
    first = jnp.where(valid, first, NEG)
    second = jnp.einsum('bhgd,sbhd->bhgs', query_head_rows.astype(jnp.float32), latest_keys.astype(jnp.float32)) / math.sqrt(HEAD_SIZE)
    second = jnp.where(jnp.arange(DECODE_STEPS, dtype=jnp.int32)[None, None, None, :] <= step_index, second, NEG)
    scores = jnp.concatenate([first, second], axis=-1)
    running_maximum = lax.optimization_barrier(jnp.max(scores, axis=-1))
    expon = jnp.exp(scores - running_maximum[..., None])
    running_total = lax.optimization_barrier(jnp.sum(expon, axis=-1))
    weights = expon.astype(jnp.bfloat16).astype(jnp.float32)
    mixed_output = jnp.einsum('bhgk,bkhd->bhgd', weights[..., :SUFFIX_SLOTS], cached_value_rows.astype(jnp.float32))
    mixed_output = mixed_output + jnp.einsum('bhgs,sbhd->bhgd', weights[..., SUFFIX_SLOTS:], latest_values.astype(jnp.float32))
    return (running_maximum, running_total, mixed_output / running_total[..., None])

def merge_parts(own_top, own_total, own_mixed, path_top, path_total, path_mixed):
    running_maximum = jnp.maximum(own_top, lax.optimization_barrier(jnp.max(path_top, axis=1)))
    own_factor = own_total * jnp.exp(own_top - running_maximum)
    path_factor = path_total * jnp.exp(path_top - running_maximum[:, None])
    numer = own_factor[..., None] * own_mixed + lax.optimization_barrier(jnp.sum(path_factor[..., None] * path_mixed.astype(jnp.float32), axis=1))
    denom = own_factor + lax.optimization_barrier(jnp.sum(path_factor, axis=1))
    result = numer / denom[..., None]
    return result.reshape(result.shape[0], QUERY_HEADS * HEAD_SIZE).astype(jnp.bfloat16)

def reference(queries, shared_prefix_keys, shared_prefix_values, row_suffix_keys, row_suffix_values, step_keys, step_values, tree_blocks, block_slot, suffix_length):
    head_group = QUERY_HEADS // KEY_VALUE_HEADS
    tile_width = 16
    row_count = DECODE_ROWS // tile_width
    key_lookup = shared_prefix_keys.reshape(N_KV, BLOCK_TOKENS, KEY_VALUE_HEADS, HEAD_SIZE)
    value_lookup = shared_prefix_values.reshape(N_KV, BLOCK_TOKENS, KEY_VALUE_HEADS, HEAD_SIZE)
    slot_indices = block_slot[tree_blocks].astype(jnp.int32)

    def one_block(operand_list):
        query_tile, cached_key_rows, cached_value_rows, latest_keys, latest_values, slot_block, lengths = operand_list
        results = []
        for step_index in range(DECODE_STEPS):
            query_head_rows = query_tile[step_index].reshape(tile_width, KEY_VALUE_HEADS, head_group, HEAD_SIZE)
            own_top, own_total, own_mixed = own_partial(query_head_rows, cached_key_rows, cached_value_rows, latest_keys, latest_values, lengths, step_index)
            tops, totals, mixes = ([], [], [])
            for entry in range(PATH_BLOCKS):
                running_maximum, running_total, mixed_output = block_partial(query_head_rows, key_lookup[slot_block[:, entry]], value_lookup[slot_block[:, entry]])
                tops.append(running_maximum)
                totals.append(running_total)
                mixes.append(mixed_output)
            results.append(merge_parts(own_top, own_total, own_mixed, jnp.stack(tops, 1), jnp.stack(totals, 1), jnp.stack(mixes, 1)))
        return jnp.stack(results)
    operand_list = (queries.reshape(DECODE_STEPS, row_count, tile_width, QUERY_HEADS * HEAD_SIZE).transpose(1, 0, 2, 3), row_suffix_keys.reshape(row_count, tile_width, SUFFIX_SLOTS, KEY_VALUE_HEADS, HEAD_SIZE), row_suffix_values.reshape(row_count, tile_width, SUFFIX_SLOTS, KEY_VALUE_HEADS, HEAD_SIZE), step_keys.reshape(DECODE_STEPS, row_count, tile_width, KEY_VALUE_HEADS, HEAD_SIZE).transpose(1, 0, 2, 3, 4), step_values.reshape(DECODE_STEPS, row_count, tile_width, KEY_VALUE_HEADS, HEAD_SIZE).transpose(1, 0, 2, 3, 4), slot_indices.reshape(row_count, tile_width, PATH_BLOCKS), suffix_length.reshape(row_count, tile_width))
    result = lax.map(one_block, operand_list)
    return result.transpose(1, 0, 2, 3).reshape(DECODE_STEPS, DECODE_ROWS, QUERY_HEADS * HEAD_SIZE)
```

```python
import functools
import math

import jax
import jax.numpy as jnp
from jax import lax
from jax.experimental import pallas as pl
from jax.experimental.pallas import tpu as pltpu
from jax.sharding import PartitionSpec as P

QUERY_HEADS = 32
KEY_VALUE_HEADS = 4
HEAD_SIZE = 128
SUFFIX_SLOTS = 32
DECODE_STEPS = 2
GROUP = QUERY_HEADS // KEY_VALUE_HEADS
WIDTH = QUERY_HEADS * HEAD_SIZE
LANES = 128

NEG = -1e30
SCALE = math.log2(math.e) / math.sqrt(HEAD_SIZE)
NT = (((1,), (1,)), ((), ()))
VMEM = 48 * 1024 * 1024


def head_columns(head):
    return slice(head * HEAD_SIZE, (head + 1) * HEAD_SIZE)


def stack_heads(query_rows, kv_head):
    return jnp.concatenate(
        [query_rows[:, head_columns(kv_head * GROUP + j)] for j in range(GROUP)], axis=0
    )


def values_and_ones(values):
    return jnp.concatenate([values, jnp.ones_like(values)], axis=1)


def attend_kernel(q_ref, k_ref, v_ref, out_ref):
    rows = q_ref.shape[0]
    lane = lax.broadcasted_iota(jnp.int32, (rows, LANES), 1)
    stats = jnp.zeros((rows, LANES), jnp.float32)
    for h in range(KEY_VALUE_HEADS):
        cols = head_columns(h)
        scores = lax.dot_general(
            stack_heads(q_ref, h), k_ref[:, cols], NT, preferred_element_type=jnp.float32
        )
        top = jnp.max(scores, axis=1, keepdims=True) * SCALE
        weights = jnp.exp2(scores * SCALE - top).astype(jnp.bfloat16)
        mixed = jnp.dot(
            weights, values_and_ones(v_ref[:, cols]), preferred_element_type=jnp.float32
        )
        total = mixed[:, HEAD_SIZE:]
        result = (mixed[:, :HEAD_SIZE] / total).astype(jnp.bfloat16)
        level = top + jnp.log2(total)
        for j in range(GROUP):
            head = h * GROUP + j
            part = slice(j * rows, (j + 1) * rows)
            out_ref[:, head_columns(head)] = result[part]
            stats = jnp.where(lane % QUERY_HEADS == head, level[part], stats)
    high = stats.astype(jnp.bfloat16).astype(jnp.float32)
    middle = (stats - high).astype(jnp.bfloat16).astype(jnp.float32)
    low = stats - high - middle
    packed = jnp.where(
        lane < QUERY_HEADS, high, jnp.where(lane < 2 * QUERY_HEADS, middle, low)
    )
    out_ref[:, WIDTH:] = packed.astype(jnp.bfloat16)


def attend(slots, keys, values, tile):
    count = slots.shape[0]
    tokens, width = keys.shape
    return pl.pallas_call(
        attend_kernel,
        grid=(count // tile,),
        in_specs=[
            pl.BlockSpec((tile, WIDTH), lambda i: (i, 0)),
            pl.BlockSpec((tokens, width), lambda i: (0, 0)),
            pl.BlockSpec((tokens, width), lambda i: (0, 0)),
        ],
        out_specs=pl.BlockSpec((tile, WIDTH + LANES), lambda i: (i, 0)),
        out_shape=jax.ShapeDtypeStruct((count, WIDTH + LANES), jnp.bfloat16),
        compiler_params=pltpu.CompilerParams(vmem_limit_bytes=VMEM),
        cost_estimate=pl.CostEstimate(
            flops=4 * count * WIDTH * tokens,
            bytes_accessed=4 * (count * WIDTH + tokens * width),
            transcendentals=count * QUERY_HEADS * tokens,
        ),
    )(slots, keys, values)


def own_kernel(q_ref, k_ref, v_ref, sk_ref, sv_ref, bias_ref, sbias_ref, out_ref, level_ref):
    rows = q_ref.shape[0]
    lane = lax.broadcasted_iota(jnp.int32, (rows, LANES), 1)
    levels = jnp.zeros((rows, LANES), jnp.float32)
    bias = jnp.concatenate([bias_ref[...]] * GROUP, axis=0)
    step_bias = jnp.concatenate([sbias_ref[...]] * GROUP, axis=0)
    for h in range(KEY_VALUE_HEADS):
        cols = head_columns(h)
        q = stack_heads(q_ref, h)
        first = lax.dot_general(q, k_ref[:, cols], NT, preferred_element_type=jnp.float32)
        second = lax.dot_general(q, sk_ref[:, cols], NT, preferred_element_type=jnp.float32)
        first = jnp.where(bias == 0, first * SCALE, NEG)
        second = jnp.where(step_bias == 0, second * SCALE, NEG)
        top = jnp.maximum(
            jnp.max(first, axis=1, keepdims=True), jnp.max(second, axis=1, keepdims=True)
        )
        mixed = jnp.dot(
            jnp.exp2(first - top).astype(jnp.bfloat16),
            values_and_ones(v_ref[:, cols]),
            preferred_element_type=jnp.float32,
        ) + jnp.dot(
            jnp.exp2(second - top).astype(jnp.bfloat16),
            values_and_ones(sv_ref[:, cols]),
            preferred_element_type=jnp.float32,
        )
        total = mixed[:, HEAD_SIZE:]
        result = mixed[:, :HEAD_SIZE] / total
        level = top + jnp.log2(total)
        for j in range(GROUP):
            head = h * GROUP + j
            part = slice(j * rows, (j + 1) * rows)
            out_ref[:, head_columns(head)] = result[part]
            levels = jnp.where(lane == head, level[part], levels)
    level_ref[...] = levels


def own_part(q, keys, values, step_keys, step_values, bias, step_bias):
    rows = q.shape[0]
    return pl.pallas_call(
        own_kernel,
        out_shape=(
            jax.ShapeDtypeStruct((rows, WIDTH), jnp.float32),
            jax.ShapeDtypeStruct((rows, LANES), jnp.float32),
        ),
        compiler_params=pltpu.CompilerParams(vmem_limit_bytes=VMEM),
        cost_estimate=pl.CostEstimate(
            flops=4 * rows * WIDTH * keys.shape[0],
            bytes_accessed=4 * keys.size,
            transcendentals=rows * QUERY_HEADS * keys.shape[0],
        ),
    )(q, keys, values, step_keys, step_values, bias, step_bias)


def merge_kernel(back_ref, place_ref, own_ref, level_ref, out_ref):
    packed = back_ref[:, WIDTH:].astype(jnp.float32).T
    path_level = (
        packed[:QUERY_HEADS]
        + packed[QUERY_HEADS : 2 * QUERY_HEADS]
        + packed[2 * QUERY_HEADS : 3 * QUERY_HEADS]
    )
    place = place_ref[...] > 0
    levels = level_ref[...]
    for head in range(QUERY_HEADS):
        cols = head_columns(head)
        own_level = levels[:, head : head + 1]
        level = jnp.where(place, path_level[head : head + 1, :], NEG)
        top = jnp.maximum(own_level, jnp.max(level, axis=1, keepdims=True))
        factor = jnp.exp2(level - top).astype(jnp.bfloat16)
        own_factor = jnp.exp2(own_level - top)
        numer = own_factor * own_ref[:, cols] + jnp.dot(
            factor, back_ref[:, cols], preferred_element_type=jnp.float32
        )
        denom = own_factor + jnp.sum(factor.astype(jnp.float32), axis=1, keepdims=True)
        out_ref[:, cols] = (numer / denom).astype(jnp.bfloat16)


def merge(back, place, own, level):
    return pl.pallas_call(
        merge_kernel,
        out_shape=jax.ShapeDtypeStruct(own.shape, jnp.bfloat16),
        compiler_params=pltpu.CompilerParams(vmem_limit_bytes=VMEM),
        cost_estimate=pl.CostEstimate(
            flops=2 * place.size * WIDTH, bytes_accessed=2 * back.size, transcendentals=0
        ),
    )(back, place, own, level)


def per_device(
    queries,
    shared_prefix_keys,
    shared_prefix_values,
    row_suffix_keys,
    row_suffix_values,
    step_keys,
    step_values,
    tree_blocks,
    block_slot,
    suffix_length,
):
    devices = lax.axis_size("kv")
    steps, rows, _ = queries.shape
    path = tree_blocks.shape[1]
    capacity = max(2, 2 * rows * path // devices)
    slots_all = devices * capacity
    blocks_flat = tree_blocks.reshape(-1)
    device_ids = jnp.arange(devices, dtype=jnp.int32)
    target = jnp.sum(
        jnp.where(blocks_flat[:, None] == device_ids[None, :], block_slot[None, :], 0), axis=1
    )
    entry = jnp.arange(rows * path, dtype=jnp.int32)
    rank = jnp.sum(
        (target[:, None] == target[None, :]) & (entry[None, :] < entry[:, None]),
        axis=1,
        dtype=jnp.int32,
    )
    slot_index = (target * capacity + rank).reshape(rows, path)
    place = jnp.sum(
        slot_index[:, :, None] == jnp.arange(slots_all, dtype=jnp.int32), axis=1
    ).astype(jnp.bfloat16)
    keys_flat = row_suffix_keys.reshape(rows * SUFFIX_SLOTS, -1)
    values_flat = row_suffix_values.reshape(rows * SUFFIX_SLOTS, -1)
    row_ids = jnp.arange(rows, dtype=jnp.int32)
    position = jnp.arange(rows * SUFFIX_SLOTS, dtype=jnp.int32)[None, :]
    bias = jnp.where(
        (position // SUFFIX_SLOTS == row_ids[:, None])
        & (position % SUFFIX_SLOTS < suffix_length[:, None]),
        0.0,
        NEG,
    )
    step_position = jnp.arange(steps * rows, dtype=jnp.int32)[None, :]
    latest_keys = step_keys.reshape(steps * rows, -1)
    latest_values = step_values.reshape(steps * rows, -1)
    tile = math.gcd(64, slots_all)
    exchange = functools.partial(
        lax.all_to_all, axis_name="kv", split_axis=0, concat_axis=0, tiled=True
    )
    received, owns, backs = [], [], []
    for t in range(steps):
        sending = lax.dot_general(
            place, queries[t], (((0,), (0,)), ((), ())), preferred_element_type=jnp.float32
        ).astype(jnp.bfloat16)
        received.append(exchange(sending.reshape(devices, capacity, WIDTH)))
    for t in range(steps):
        step_bias = jnp.where(
            (step_position % rows == row_ids[:, None]) & (step_position // rows <= t), 0.0, NEG
        )
        owns.append(
            own_part(
                queries[t], keys_flat, values_flat, latest_keys, latest_values, bias, step_bias
            )
        )
    for t in range(steps):
        result = attend(
            received[t].reshape(slots_all, WIDTH), shared_prefix_keys, shared_prefix_values, tile
        )
        backs.append(exchange(result.reshape(devices, capacity, WIDTH + LANES)))
    return jnp.stack(
        [
            merge(backs[t].reshape(slots_all, WIDTH + LANES), place, *owns[t])
            for t in range(steps)
        ]
    )


def solution(mesh):
    return jax.shard_map(
        per_device,
        mesh=mesh,
        in_specs=(
            P(None, ("groups", "kv"), None),
            P("kv", None),
            P("kv", None),
            P(("groups", "kv"), None, None),
            P(("groups", "kv"), None, None),
            P(None, ("groups", "kv"), None),
            P(None, ("groups", "kv"), None),
            P(("groups", "kv"), None),
            P(),
            P(("groups", "kv")),
        ),
        out_specs=P(None, ("groups", "kv"), None),
        check_vma=False,
    )
```

```python
import functools
import math

import jax
import jax.numpy as jnp
from jax import lax
from jax.experimental import pallas as pl
from jax.experimental.pallas import tpu as pltpu
from jax.sharding import PartitionSpec as P

QUERY_HEADS = 32
KEY_VALUE_HEADS = 4
HEAD_SIZE = 128
SUFFIX_SLOTS = 32
DECODE_STEPS = 2
GROUP = QUERY_HEADS // KEY_VALUE_HEADS
WIDTH = QUERY_HEADS * HEAD_SIZE
LANES = 128

NEG = -1e30
SCALE = math.log2(math.e) / math.sqrt(HEAD_SIZE)
NT = (((1,), (1,)), ((), ()))
VMEM = 48 * 1024 * 1024


def head_columns(head):
    return slice(head * HEAD_SIZE, (head + 1) * HEAD_SIZE)


def stack_heads(query_rows, kv_head):
    return jnp.concatenate(
        [query_rows[:, head_columns(kv_head * GROUP + j)] for j in range(GROUP)], axis=0
    )


def values_and_ones(values):
    return jnp.concatenate([values, jnp.ones_like(values)], axis=1)


def attend_kernel(q_ref, k_ref, v_ref, out_ref):
    rows = q_ref.shape[0]
    lane = lax.broadcasted_iota(jnp.int32, (rows, LANES), 1)
    stats = jnp.zeros((rows, LANES), jnp.float32)
    for h in range(KEY_VALUE_HEADS):
        cols = head_columns(h)
        scores = lax.dot_general(
            stack_heads(q_ref, h), k_ref[:, cols], NT, preferred_element_type=jnp.float32
        )
        top = jnp.max(scores, axis=1, keepdims=True) * SCALE
        weights = jnp.exp2(scores * SCALE - top).astype(jnp.bfloat16)
        mixed = jnp.dot(
            weights, values_and_ones(v_ref[:, cols]), preferred_element_type=jnp.float32
        )
        total = mixed[:, HEAD_SIZE:]
        result = (mixed[:, :HEAD_SIZE] / total).astype(jnp.bfloat16)
        level = top + jnp.log2(total)
        for j in range(GROUP):
            head = h * GROUP + j
            part = slice(j * rows, (j + 1) * rows)
            out_ref[:, head_columns(head)] = result[part]
            stats = jnp.where(lane % QUERY_HEADS == head, level[part], stats)
    high = stats.astype(jnp.bfloat16).astype(jnp.float32)
    middle = (stats - high).astype(jnp.bfloat16).astype(jnp.float32)
    low = stats - high - middle
    packed = jnp.where(
        lane < QUERY_HEADS, high, jnp.where(lane < 2 * QUERY_HEADS, middle, low)
    )
    out_ref[:, WIDTH:] = packed.astype(jnp.bfloat16)


def attend(slots, keys, values, tile):
    count = slots.shape[0]
    tokens, width = keys.shape
    return pl.pallas_call(
        attend_kernel,
        grid=(count // tile,),
        in_specs=[
            pl.BlockSpec((tile, WIDTH), lambda i: (i, 0)),
            pl.BlockSpec((tokens, width), lambda i: (0, 0)),
            pl.BlockSpec((tokens, width), lambda i: (0, 0)),
        ],
        out_specs=pl.BlockSpec((tile, WIDTH + LANES), lambda i: (i, 0)),
        out_shape=jax.ShapeDtypeStruct((count, WIDTH + LANES), jnp.bfloat16),
        compiler_params=pltpu.CompilerParams(vmem_limit_bytes=VMEM),
        cost_estimate=pl.CostEstimate(
            flops=4 * count * WIDTH * tokens,
            bytes_accessed=4 * (count * WIDTH + tokens * width),
            transcendentals=count * QUERY_HEADS * tokens,
        ),
    )(slots, keys, values)


def own_kernel(q_ref, k_ref, v_ref, sk_ref, sv_ref, bias_ref, sbias_ref, out_ref, level_ref):
    rows = q_ref.shape[0]
    lane = lax.broadcasted_iota(jnp.int32, (rows, LANES), 1)
    levels = jnp.zeros((rows, LANES), jnp.float32)
    bias = jnp.concatenate([bias_ref[...]] * GROUP, axis=0)
    step_bias = jnp.concatenate([sbias_ref[...]] * GROUP, axis=0)
    for h in range(KEY_VALUE_HEADS):
        cols = head_columns(h)
        q = stack_heads(q_ref, h)
        first = lax.dot_general(q, k_ref[:, cols], NT, preferred_element_type=jnp.float32)
        second = lax.dot_general(q, sk_ref[:, cols], NT, preferred_element_type=jnp.float32)
        first = jnp.where(bias == 0, first * SCALE, NEG)
        second = jnp.where(step_bias == 0, second * SCALE, NEG)
        top = jnp.maximum(
            jnp.max(first, axis=1, keepdims=True), jnp.max(second, axis=1, keepdims=True)
        )
        mixed = jnp.dot(
            jnp.exp2(first - top).astype(jnp.bfloat16),
            values_and_ones(v_ref[:, cols]),
            preferred_element_type=jnp.float32,
        ) + jnp.dot(
            jnp.exp2(second - top).astype(jnp.bfloat16),
            values_and_ones(sv_ref[:, cols]),
            preferred_element_type=jnp.float32,
        )
        total = mixed[:, HEAD_SIZE:]
        result = mixed[:, :HEAD_SIZE] / total
        level = top + jnp.log2(total)
        for j in range(GROUP):
            head = h * GROUP + j
            part = slice(j * rows, (j + 1) * rows)
            out_ref[:, head_columns(head)] = result[part]
            levels = jnp.where(lane == head, level[part], levels)
    level_ref[...] = levels


def own_part(q, keys, values, step_keys, step_values, bias, step_bias):
    rows = q.shape[0]
    return pl.pallas_call(
        own_kernel,
        out_shape=(
            jax.ShapeDtypeStruct((rows, WIDTH), jnp.float32),
            jax.ShapeDtypeStruct((rows, LANES), jnp.float32),
        ),
        compiler_params=pltpu.CompilerParams(vmem_limit_bytes=VMEM),
        cost_estimate=pl.CostEstimate(
            flops=4 * rows * WIDTH * keys.shape[0],
            bytes_accessed=4 * keys.size,
            transcendentals=rows * QUERY_HEADS * keys.shape[0],
        ),
    )(q, keys, values, step_keys, step_values, bias, step_bias)


def merge_kernel(back_ref, place_ref, own_ref, level_ref, out_ref):
    packed = back_ref[:, WIDTH:].astype(jnp.float32).T
    path_level = (
        packed[:QUERY_HEADS]
        + packed[QUERY_HEADS : 2 * QUERY_HEADS]
        + packed[2 * QUERY_HEADS : 3 * QUERY_HEADS]
    )
    place = place_ref[...] > 0
    levels = level_ref[...]
    for head in range(QUERY_HEADS):
        cols = head_columns(head)
        own_level = levels[:, head : head + 1]
        level = jnp.where(place, path_level[head : head + 1, :], NEG)
        top = jnp.maximum(own_level, jnp.max(level, axis=1, keepdims=True))
        factor = jnp.exp2(level - top).astype(jnp.bfloat16)
        own_factor = jnp.exp2(own_level - top)
        numer = own_factor * own_ref[:, cols] + jnp.dot(
            factor, back_ref[:, cols], preferred_element_type=jnp.float32
        )
        denom = own_factor + jnp.sum(factor.astype(jnp.float32), axis=1, keepdims=True)
        out_ref[:, cols] = (numer / denom).astype(jnp.bfloat16)


def merge(back, place, own, level):
    return pl.pallas_call(
        merge_kernel,
        out_shape=jax.ShapeDtypeStruct(own.shape, jnp.bfloat16),
        compiler_params=pltpu.CompilerParams(vmem_limit_bytes=VMEM),
        cost_estimate=pl.CostEstimate(
            flops=2 * place.size * WIDTH, bytes_accessed=2 * back.size, transcendentals=0
        ),
    )(back, place, own, level)


def exchange_masks(devices, turn):
    masks = [1 << b for b in reversed(range((devices - 1).bit_length()))]
    if turn % 2 and 2 in masks:
        masks.remove(2)
        masks.insert(0, 2)
    return masks


def gather_rows(block, devices, masks):
    order, held = [0], block
    for mask in masks:
        partner = lax.ppermute(held, "kv", [(i, i ^ mask) for i in range(devices)])
        held = jnp.concatenate([held, partner], axis=0)
        order = order + [o ^ mask for o in order]
    return order, held


def per_device(
    queries,
    shared_prefix_keys,
    shared_prefix_values,
    row_suffix_keys,
    row_suffix_values,
    step_keys,
    step_values,
    tree_blocks,
    block_slot,
    suffix_length,
):
    devices = lax.axis_size("kv")
    steps, rows, _ = queries.shape
    path = tree_blocks.shape[1]
    capacity = max(2, 2 * rows * path // devices)
    slots_all = devices * capacity
    blocks_flat = tree_blocks.reshape(-1)
    device_ids = jnp.arange(devices, dtype=jnp.int32)
    target = jnp.sum(
        jnp.where(blocks_flat[:, None] == device_ids[None, :], block_slot[None, :], 0), axis=1
    )
    entry = jnp.arange(rows * path, dtype=jnp.int32)
    rank = jnp.sum(
        (target[:, None] == target[None, :]) & (entry[None, :] < entry[:, None]),
        axis=1,
        dtype=jnp.int32,
    )
    slot_index = (target * capacity + rank).reshape(rows, path)
    place = jnp.sum(
        slot_index[:, :, None] == jnp.arange(slots_all, dtype=jnp.int32), axis=1
    ).astype(jnp.bfloat16)
    keys_flat = row_suffix_keys.reshape(rows * SUFFIX_SLOTS, -1)
    values_flat = row_suffix_values.reshape(rows * SUFFIX_SLOTS, -1)
    row_ids = jnp.arange(rows, dtype=jnp.int32)
    position = jnp.arange(rows * SUFFIX_SLOTS, dtype=jnp.int32)[None, :]
    bias = jnp.where(
        (position // SUFFIX_SLOTS == row_ids[:, None])
        & (position % SUFFIX_SLOTS < suffix_length[:, None]),
        0.0,
        NEG,
    )
    step_position = jnp.arange(steps * rows, dtype=jnp.int32)[None, :]
    latest_keys = step_keys.reshape(steps * rows, -1)
    latest_values = step_values.reshape(steps * rows, -1)
    tile = math.gcd(64, slots_all)
    exchange = functools.partial(
        lax.all_to_all, axis_name="kv", split_axis=0, concat_axis=0, tiled=True
    )
    received, owns, backs = [], [], []
    if 4 * capacity >= rows and devices & (devices - 1) == 0:
        me = lax.axis_index("kv")
        everyone = lax.all_gather(slot_index, "kv", axis=0)
        wanted = me * capacity + jnp.arange(capacity, dtype=jnp.int32)
        filled = jnp.any(everyone[:, None, :, :] == wanted[None, :, None, None], axis=3)
        for t in range(steps):
            order, gathered = gather_rows(queries[t], devices, exchange_masks(devices, t))
            sender = jnp.asarray(order, jnp.int32) ^ me
            chosen = (
                filled[:, :, None, :] & (device_ids[:, None] == sender[None, :])[:, None, :, None]
            ).astype(jnp.bfloat16)
            received.append(
                jnp.dot(
                    chosen.reshape(slots_all, devices * rows),
                    gathered,
                    preferred_element_type=jnp.float32,
                ).astype(jnp.bfloat16)
            )
    else:
        for t in range(steps):
            sending = lax.dot_general(
                place, queries[t], (((0,), (0,)), ((), ())), preferred_element_type=jnp.float32
            ).astype(jnp.bfloat16)
            tiles = exchange(sending.reshape(devices, capacity, WIDTH))
            received.append(tiles.reshape(slots_all, WIDTH))
    for t in range(steps):
        step_bias = jnp.where(
            (step_position % rows == row_ids[:, None]) & (step_position // rows <= t), 0.0, NEG
        )
        owns.append(
            own_part(
                queries[t], keys_flat, values_flat, latest_keys, latest_values, bias, step_bias
            )
        )
    for t in range(steps):
        result = attend(
            received[t], shared_prefix_keys, shared_prefix_values, tile
        )
        backs.append(exchange(result.reshape(devices, capacity, WIDTH + LANES)))
    return jnp.stack(
        [
            merge(backs[t].reshape(slots_all, WIDTH + LANES), place, *owns[t])
            for t in range(steps)
        ]
    )


def solution(mesh):
    return jax.shard_map(
        per_device,
        mesh=mesh,
        in_specs=(
            P(None, ("groups", "kv"), None),
            P("kv", None),
            P("kv", None),
            P(("groups", "kv"), None, None),
            P(("groups", "kv"), None, None),
            P(None, ("groups", "kv"), None),
            P(None, ("groups", "kv"), None),
            P(("groups", "kv"), None),
            P(),
            P(("groups", "kv")),
        ),
        out_specs=P(None, ("groups", "kv"), None),
        check_vma=False,
    )
```

```python
import functools
import math

import jax
import jax.numpy as jnp
from jax import lax
from jax.experimental import pallas as pl
from jax.experimental.pallas import tpu as pltpu
from jax.sharding import PartitionSpec as P

QUERY_HEADS = 32
KEY_VALUE_HEADS = 4
HEAD_SIZE = 128
SUFFIX_SLOTS = 32
DECODE_STEPS = 2
GROUP = QUERY_HEADS // KEY_VALUE_HEADS
WIDTH = QUERY_HEADS * HEAD_SIZE
LANES = 128

NEG = -1e30
SCALE = math.log2(math.e) / math.sqrt(HEAD_SIZE)
NT = (((1,), (1,)), ((), ()))
VMEM = 48 * 1024 * 1024


def head_columns(head):
    return slice(head * HEAD_SIZE, (head + 1) * HEAD_SIZE)


def stack_heads(query_rows, kv_head):
    return jnp.concatenate(
        [query_rows[:, head_columns(kv_head * GROUP + j)] for j in range(GROUP)], axis=0
    )


def values_and_ones(values):
    return jnp.concatenate([values, jnp.ones_like(values)], axis=1)


def attend_kernel(q_ref, k_ref, v_ref, out_ref):
    rows = q_ref.shape[0]
    lane = lax.broadcasted_iota(jnp.int32, (rows, LANES), 1)
    stats = jnp.zeros((rows, LANES), jnp.float32)
    for h in range(KEY_VALUE_HEADS):
        cols = head_columns(h)
        scores = lax.dot_general(
            stack_heads(q_ref, h), k_ref[:, cols], NT, preferred_element_type=jnp.float32
        )
        top = jnp.max(scores, axis=1, keepdims=True) * SCALE
        weights = jnp.exp2(scores * SCALE - top).astype(jnp.bfloat16)
        mixed = jnp.dot(
            weights, values_and_ones(v_ref[:, cols]), preferred_element_type=jnp.float32
        )
        total = mixed[:, HEAD_SIZE:]
        result = (mixed[:, :HEAD_SIZE] / total).astype(jnp.bfloat16)
        level = top + jnp.log2(total)
        for j in range(GROUP):
            head = h * GROUP + j
            part = slice(j * rows, (j + 1) * rows)
            out_ref[:, head_columns(head)] = result[part]
            stats = jnp.where(lane % QUERY_HEADS == head, level[part], stats)
    high = stats.astype(jnp.bfloat16).astype(jnp.float32)
    middle = (stats - high).astype(jnp.bfloat16).astype(jnp.float32)
    low = stats - high - middle
    packed = jnp.where(
        lane < QUERY_HEADS, high, jnp.where(lane < 2 * QUERY_HEADS, middle, low)
    )
    out_ref[:, WIDTH:] = packed.astype(jnp.bfloat16)


def attend(slots, keys, values, tile):
    count = slots.shape[0]
    tokens, width = keys.shape
    return pl.pallas_call(
        attend_kernel,
        grid=(count // tile,),
        in_specs=[
            pl.BlockSpec((tile, WIDTH), lambda i: (i, 0)),
            pl.BlockSpec((tokens, width), lambda i: (0, 0)),
            pl.BlockSpec((tokens, width), lambda i: (0, 0)),
        ],
        out_specs=pl.BlockSpec((tile, WIDTH + LANES), lambda i: (i, 0)),
        out_shape=jax.ShapeDtypeStruct((count, WIDTH + LANES), jnp.bfloat16),
        compiler_params=pltpu.CompilerParams(vmem_limit_bytes=VMEM),
        cost_estimate=pl.CostEstimate(
            flops=4 * count * WIDTH * tokens,
            bytes_accessed=4 * (count * WIDTH + tokens * width),
            transcendentals=count * QUERY_HEADS * tokens,
        ),
    )(slots, keys, values)


def own_kernel(q_ref, k_ref, v_ref, sk_ref, sv_ref, bias_ref, sbias_ref, out_ref, level_ref):
    rows = q_ref.shape[0]
    lane = lax.broadcasted_iota(jnp.int32, (rows, LANES), 1)
    levels = jnp.zeros((rows, LANES), jnp.float32)
    bias = jnp.concatenate([bias_ref[...]] * GROUP, axis=0)
    step_bias = jnp.concatenate([sbias_ref[...]] * GROUP, axis=0)
    for h in range(KEY_VALUE_HEADS):
        cols = head_columns(h)
        q = stack_heads(q_ref, h)
        first = lax.dot_general(q, k_ref[:, cols], NT, preferred_element_type=jnp.float32)
        second = lax.dot_general(q, sk_ref[:, cols], NT, preferred_element_type=jnp.float32)
        first = jnp.where(bias == 0, first * SCALE, NEG)
        second = jnp.where(step_bias == 0, second * SCALE, NEG)
        top = jnp.maximum(
            jnp.max(first, axis=1, keepdims=True), jnp.max(second, axis=1, keepdims=True)
        )
        mixed = jnp.dot(
            jnp.exp2(first - top).astype(jnp.bfloat16),
            values_and_ones(v_ref[:, cols]),
            preferred_element_type=jnp.float32,
        ) + jnp.dot(
            jnp.exp2(second - top).astype(jnp.bfloat16),
            values_and_ones(sv_ref[:, cols]),
            preferred_element_type=jnp.float32,
        )
        total = mixed[:, HEAD_SIZE:]
        result = mixed[:, :HEAD_SIZE] / total
        level = top + jnp.log2(total)
        for j in range(GROUP):
            head = h * GROUP + j
            part = slice(j * rows, (j + 1) * rows)
            out_ref[:, head_columns(head)] = result[part]
            levels = jnp.where(lane == head, level[part], levels)
    level_ref[...] = levels


def own_part(q, keys, values, step_keys, step_values, bias, step_bias):
    rows = q.shape[0]
    return pl.pallas_call(
        own_kernel,
        out_shape=(
            jax.ShapeDtypeStruct((rows, WIDTH), jnp.float32),
            jax.ShapeDtypeStruct((rows, LANES), jnp.float32),
        ),
        compiler_params=pltpu.CompilerParams(vmem_limit_bytes=VMEM),
        cost_estimate=pl.CostEstimate(
            flops=4 * rows * WIDTH * keys.shape[0],
            bytes_accessed=4 * keys.size,
            transcendentals=rows * QUERY_HEADS * keys.shape[0],
        ),
    )(q, keys, values, step_keys, step_values, bias, step_bias)


def merge_kernel(back_ref, place_ref, own_ref, level_ref, out_ref):
    packed = back_ref[:, WIDTH:].astype(jnp.float32).T
    path_level = (
        packed[:QUERY_HEADS]
        + packed[QUERY_HEADS : 2 * QUERY_HEADS]
        + packed[2 * QUERY_HEADS : 3 * QUERY_HEADS]
    )
    place = place_ref[...] > 0
    levels = level_ref[...]
    for head in range(QUERY_HEADS):
        cols = head_columns(head)
        own_level = levels[:, head : head + 1]
        level = jnp.where(place, path_level[head : head + 1, :], NEG)
        top = jnp.maximum(own_level, jnp.max(level, axis=1, keepdims=True))
        factor = jnp.exp2(level - top).astype(jnp.bfloat16)
        own_factor = jnp.exp2(own_level - top)
        numer = own_factor * own_ref[:, cols] + jnp.dot(
            factor, back_ref[:, cols], preferred_element_type=jnp.float32
        )
        denom = own_factor + jnp.sum(factor.astype(jnp.float32), axis=1, keepdims=True)
        out_ref[:, cols] = (numer / denom).astype(jnp.bfloat16)


def merge(back, place, own, level):
    return pl.pallas_call(
        merge_kernel,
        out_shape=jax.ShapeDtypeStruct(own.shape, jnp.bfloat16),
        compiler_params=pltpu.CompilerParams(vmem_limit_bytes=VMEM),
        cost_estimate=pl.CostEstimate(
            flops=2 * place.size * WIDTH, bytes_accessed=2 * back.size, transcendentals=0
        ),
    )(back, place, own, level)


def exchange_masks(devices, turn):
    masks = [1 << b for b in reversed(range((devices - 1).bit_length()))]
    if turn % 2 and 2 in masks:
        masks.remove(2)
        masks.insert(0, 2)
    return masks


def gather_rows(block, devices, masks):
    order, held = [0], block
    for mask in masks:
        partner = lax.ppermute(held, "kv", [(i, i ^ mask) for i in range(devices)])
        held = jnp.concatenate([held, partner], axis=0)
        order = order + [o ^ mask for o in order]
    return order, held


def per_device(
    queries,
    shared_prefix_keys,
    shared_prefix_values,
    row_suffix_keys,
    row_suffix_values,
    step_keys,
    step_values,
    tree_blocks,
    block_slot,
    suffix_length,
):
    devices = lax.axis_size("kv")
    steps, rows, _ = queries.shape
    path = tree_blocks.shape[1]
    capacity = max(2, 2 * rows * path // devices)
    slots_all = devices * capacity
    blocks_flat = tree_blocks.reshape(-1)
    device_ids = jnp.arange(devices, dtype=jnp.int32)
    target = jnp.sum(
        jnp.where(blocks_flat[:, None] == device_ids[None, :], block_slot[None, :], 0), axis=1
    )
    entry = jnp.arange(rows * path, dtype=jnp.int32)
    rank = jnp.sum(
        (target[:, None] == target[None, :]) & (entry[None, :] < entry[:, None]),
        axis=1,
        dtype=jnp.int32,
    )
    slot_index = (target * capacity + rank).reshape(rows, path)
    place = jnp.sum(
        slot_index[:, :, None] == jnp.arange(slots_all, dtype=jnp.int32), axis=1
    ).astype(jnp.bfloat16)
    keys_flat = row_suffix_keys.reshape(rows * SUFFIX_SLOTS, -1)
    values_flat = row_suffix_values.reshape(rows * SUFFIX_SLOTS, -1)
    row_ids = jnp.arange(rows, dtype=jnp.int32)
    position = jnp.arange(rows * SUFFIX_SLOTS, dtype=jnp.int32)[None, :]
    bias = jnp.where(
        (position // SUFFIX_SLOTS == row_ids[:, None])
        & (position % SUFFIX_SLOTS < suffix_length[:, None]),
        0.0,
        NEG,
    )
    step_position = jnp.arange(steps * rows, dtype=jnp.int32)[None, :]
    latest_keys = step_keys.reshape(steps * rows, -1)
    latest_values = step_values.reshape(steps * rows, -1)
    tile = math.gcd(64, slots_all)
    exchange = functools.partial(
        lax.all_to_all, axis_name="kv", split_axis=0, concat_axis=0, tiled=True
    )
    received, owns, backs = [], [], []
    if 4 * capacity >= rows and devices & (devices - 1) == 0 and max(devices, capacity) <= 256:
        me = lax.axis_index("kv")
        labels = jnp.concatenate([target.reshape(rows, path), rank.reshape(rows, path)], axis=1)
        labels = jnp.pad(labels, ((0, 0), (0, LANES - 2 * path))).astype(jnp.bfloat16)
        ranks = jnp.arange(capacity, dtype=jnp.int32)[None, :, None, None]
        for t in range(steps):
            order, gathered = gather_rows(
                jnp.concatenate([queries[t], labels], axis=1),
                devices,
                exchange_masks(devices, t),
            )
            named = gathered[:, WIDTH : WIDTH + 2 * path].astype(jnp.int32)
            named = named.reshape(devices, 1, rows, 2 * path)
            filled = jnp.any((named[..., :path] == me) & (named[..., path:] == ranks), axis=3)
            sender = jnp.asarray(order, jnp.int32) ^ me
            chosen = (
                filled.transpose(1, 0, 2)[None]
                & (device_ids[:, None] == sender[None, :])[:, None, :, None]
            ).astype(jnp.bfloat16)
            received.append(
                jnp.dot(
                    chosen.reshape(slots_all, devices * rows),
                    gathered,
                    preferred_element_type=jnp.float32,
                ).astype(jnp.bfloat16)
            )
    else:
        for t in range(steps):
            sending = lax.dot_general(
                place, queries[t], (((0,), (0,)), ((), ())), preferred_element_type=jnp.float32
            ).astype(jnp.bfloat16)
            tiles = exchange(sending.reshape(devices, capacity, WIDTH))
            received.append(tiles.reshape(slots_all, WIDTH))
    for t in range(steps):
        step_bias = jnp.where(
            (step_position % rows == row_ids[:, None]) & (step_position // rows <= t), 0.0, NEG
        )
        owns.append(
            own_part(
                queries[t], keys_flat, values_flat, latest_keys, latest_values, bias, step_bias
            )
        )
    for t in range(steps):
        result = attend(
            received[t], shared_prefix_keys, shared_prefix_values, tile
        )
        backs.append(exchange(result.reshape(devices, capacity, WIDTH + LANES)))
    return jnp.stack(
        [
            merge(backs[t].reshape(slots_all, WIDTH + LANES), place, *owns[t])
            for t in range(steps)
        ]
    )


def solution(mesh):
    return jax.shard_map(
        per_device,
        mesh=mesh,
        in_specs=(
            P(None, ("groups", "kv"), None),
            P("kv", None),
            P("kv", None),
            P(("groups", "kv"), None, None),
            P(("groups", "kv"), None, None),
            P(None, ("groups", "kv"), None),
            P(None, ("groups", "kv"), None),
            P(("groups", "kv"), None),
            P(),
            P(("groups", "kv")),
        ),
        out_specs=P(None, ("groups", "kv"), None),
        check_vma=False,
    )
```
